256 devices in a mesh: wa: 8 (over z), vert: 32 (over y, x, core).
Axes of the slice: x: 4, y: 4, z: 8, core: 2. Of those that a mesh axis runs over, the one named last changes fastest.
Arguments:
- hidden_in: bfloat16 [384, 8192], P(None, 'wa')
- gate_levels: bfloat16 [8192, 28672], P('wa', 'vert'), may hold values from -127 to 127, as said below
- up_levels: bfloat16 [8192, 28672], P('wa', 'vert'), may hold values from -127 to 127, as said below
- gate_scale: float32 [28672], P('vert'), as said below
- up_scale: float32 [28672], P('vert'), as said below
- down_levels: bfloat16 [28672, 8192], P('vert', 'wa'), may hold values from -127 to 127, as said below
- down_scale: float32 [8192], P('wa'), as said below
- norm_gain: float32 [8192], P('wa'), may hold values from 0.5 to 1.5
- head_weight: bfloat16 [8192, 16000], P('wa', 'vert')
- reward_states: bfloat16 [8, 384, 4096], P('wa', None, 'vert'), may hold values from -6 to 6
- reward_gain: float32 [8, 4096], P('wa'), may hold values from 0.5 to 1.5
- reward_heads: bfloat16 [8, 4096, 16000], P('wa', None, 'vert')
- preference: int32 [384, 8], P(None, 'wa'), may hold values from 0 to 16
- token_ids: int32 [384], P('wa'), may hold values from 0 to 15999
Outputs:
- log_probs: float32 [384, 16000], P('wa', 'vert')
- chosen: float32 [384], P('wa')
The draws below stay inside these ranges and needn't reach their ends.
Inputs may be any that keep to these rules, and one draw needn't show every extreme that they name: `gate_levels`: whole numbers. `up_levels`: whole numbers. `down_levels`: whole numbers. `gate_scale`: positive. `up_scale`: positive. `down_scale`: positive.
All inputs are finite; a program needn't handle non-finite values.
Results may differ from the reference program's by a relative error of at most 0.0025.
Values may be sent and summed in bfloat16 or wider, within the bound.
No kernel may reach another device: no remote copies, remote signals or barrier semaphores. Data moves between devices by JAX's collectives and lax.ppermute only.
A program may use at most 64 MiB of HBM per device.

```python
import math
import jax
import jax.numpy as jnp
import numpy as np
from jax import lax

D = 8192
FF = 28672
RD = 4096
VOCAB = 16000
ROWS = 384
REWARDS = 8


def level_table(key, salt, rows, cols):
    values = jax.random.randint(jax.random.fold_in(key, salt), (rows, cols), -127, 128)
    return values.astype(jnp.float32).astype(jnp.bfloat16)


def scale_table(key, salt, count, unit):
    logs = jax.random.uniform(jax.random.fold_in(key, salt), (count,), jnp.float32, math.log(0.5), math.log(2.0))
    return (jnp.exp(logs) * unit).astype(jnp.float32)


def head_table(key, salt, lead, fan, vocab):
    base_key = jax.random.fold_in(key, salt)
    ramp = 1.0 + 0.7 * jnp.arange(vocab, dtype=jnp.float32) / max(vocab - 1, 1)
    weight = jax.random.normal(jax.random.fold_in(base_key, 1), (lead, fan, vocab), jnp.float32) * (3.0 / math.sqrt(fan)) * ramp
    return weight


def draw_hidden_in(key, part):
    ramp = 1.0 + 2.0 * jnp.arange(D, dtype=jnp.float32) / max(D - 1, 1)
    values = jax.random.normal(jax.random.fold_in(key, 21), (ROWS, D), jnp.float32)
    return (values * ramp).astype(jnp.bfloat16)


def draw_gate_levels(key, part):
    return level_table(key, 31, D, FF)


def draw_up_levels(key, part):
    return level_table(key, 32, D, FF)


def draw_down_levels(key, part):
    return level_table(key, 33, FF, D)


def draw_gate_scale(key, part):
    return scale_table(key, 41, FF, 1.0 / (73.6 * 2.08 * math.sqrt(D)))


def draw_up_scale(key, part):
    return scale_table(key, 42, FF, 1.0 / (73.6 * 2.08 * math.sqrt(D)))


def draw_down_scale(key, part):
    return scale_table(key, 43, D, 1.0 / (73.6 * 0.8 * math.sqrt(FF)))


def draw_head_weight(key, part):
    return head_table(key, 51, 1, D, VOCAB)[0].astype(jnp.bfloat16)


def draw_reward_heads(key, part):
    return head_table(key, 52, REWARDS, RD, VOCAB).astype(jnp.bfloat16)


def place_ends(entries, key, low, largest):
    shape = entries.shape
    index_at = [jax.random.randint(jax.random.fold_in(key, axis), (), 0, shape[axis]) for axis in range(len(shape))]
    entries = entries.at[tuple(index_at)].set(low)
    longest = shape.index(max(shape))
    index_at[longest] = (index_at[longest] + 1) % shape[longest]
    return entries.at[tuple(index_at)].set(largest)


def block_levels(stream_key, shape, split, least, high):
    level, own = 1.0, jax.random.fold_in(stream_key, 6)
    for axis_at, blocks in split:
        steps = jnp.exp(jax.random.uniform(jax.random.fold_in(own, axis_at), (blocks,), jnp.float32, least / len(split), high / len(split)))
        level = level * jnp.repeat(steps, shape[axis_at] // blocks).reshape([-1 if axis == axis_at else 1 for axis in range(len(shape))])
    return level


def cumulative_ranks(amount, skew):
    loads = [(1 << 20) // math.isqrt(standing ** skew) + 1 for standing in range(1, amount + 1)]
    scale = 1 + sum(loads) // (1 << 30)
    return np.cumsum(np.array([max(1, weight // scale) for weight in loads]))


def ranked_ids(rng, shape, amount, lean):
    table = cumulative_ranks(amount, lean)
    pick = jax.random.randint(jax.random.fold_in(rng, 1), shape, 0, int(table[amount - 1]))
    rank = jnp.searchsorted(jnp.asarray(table, jnp.int32), pick, side="right")
    return jax.random.permutation(jax.random.fold_in(rng, 2), amount)[rank].astype(jnp.int32)


def noise(stream_key, shape, spread, limit, cuts=(), kind=jnp.bfloat16):
    drawn = spread * jax.random.normal(stream_key, shape, jnp.float32)
    if cuts:
        drawn = drawn * block_levels(stream_key, shape, cuts, -0.22, 0.18)
    return jnp.clip(drawn, -limit, limit).astype(kind)


def setup_inputs(seed: int = 0) -> dict:
    streams_of = jax.random.split(jax.random.key(seed), 15)
    return {
        "hidden_in": draw_hidden_in(jax.random.fold_in(streams_of[14], 71), 0),
        "gate_levels": draw_gate_levels(jax.random.fold_in(streams_of[14], 71), 0),
        "up_levels": draw_up_levels(jax.random.fold_in(streams_of[14], 71), 0),
        "gate_scale": draw_gate_scale(jax.random.fold_in(streams_of[14], 71), 0),
        "up_scale": draw_up_scale(jax.random.fold_in(streams_of[14], 71), 0),
        "down_levels": draw_down_levels(jax.random.fold_in(streams_of[14], 71), 0),
        "down_scale": draw_down_scale(jax.random.fold_in(streams_of[14], 71), 0),
        "norm_gain": jnp.clip(1.0 + 0.1 * jax.random.normal(streams_of[7], (D,), jnp.float32), 0.5, 1.5),
        "head_weight": draw_head_weight(jax.random.fold_in(streams_of[14], 71), 0),
        "reward_states": noise(streams_of[9], (REWARDS, ROWS, RD), 1.0, 6.0, ((0, 8), (2, 32))),
        "reward_gain": jnp.clip(1.0 + 0.1 * jax.random.normal(streams_of[10], (REWARDS, RD), jnp.float32), 0.5, 1.5),
        "reward_heads": draw_reward_heads(jax.random.fold_in(streams_of[14], 71), 0),
        "preference": place_ends(jax.random.randint(streams_of[12], (ROWS, REWARDS), 0, 17), jax.random.fold_in(streams_of[12], 1), 0, 16).astype(jnp.int32),
        "token_ids": place_ends(ranked_ids(streams_of[13], (ROWS,), VOCAB, 2), jax.random.fold_in(streams_of[13], 3), 0, VOCAB - 1).astype(jnp.int32),
    }


def log_softmax_rows(values):
    top = lax.optimization_barrier(jnp.max(values, axis=1, keepdims=True))
    return values - top - jnp.log(lax.optimization_barrier(jnp.sum(jnp.exp(values - top), axis=1, keepdims=True)))

def reference(hidden_in, gate_levels, up_levels, gate_scale, up_scale, down_levels, down_scale, norm_gain, head_weight, reward_states, reward_gain, reward_heads, preference, token_ids):
    gate = jnp.dot(hidden_in, gate_levels, preferred_element_type=jnp.float32) * gate_scale
    up = jnp.dot(hidden_in, up_levels, preferred_element_type=jnp.float32) * up_scale
    hidden = (jax.nn.silu(gate) * up).astype(jnp.bfloat16)
    down = jnp.dot(hidden, down_levels, preferred_element_type=jnp.float32) * down_scale
    resid = hidden_in.astype(jnp.float32) + down
    normed = (resid * lax.rsqrt(lax.optimization_barrier(jnp.mean(resid * resid, axis=1, keepdims=True)) + 1e-05) * norm_gain).astype(jnp.bfloat16)
    base = jnp.dot(normed, head_weight, preferred_element_type=jnp.float32)
    base_logp = log_softmax_rows(base)
    weights = preference.astype(jnp.float32).T / 16.0

    def one_reward(packed):
        states, gain, head, weight = packed
        values = states.astype(jnp.float32)
        scaled = (values * lax.rsqrt(lax.optimization_barrier(jnp.mean(values * values, axis=1, keepdims=True)) + 1e-05) * gain).astype(jnp.bfloat16)
        logits = jnp.dot(scaled, head, preferred_element_type=jnp.float32)
        return weight[:, None] * log_softmax_rows(logits)
    terms = lax.map(one_reward, (reward_states, reward_gain, reward_heads, weights))
    mix = base_logp + lax.optimization_barrier(jnp.sum(terms, axis=0))
    log_probs = log_softmax_rows(mix)
    chosen = jnp.take_along_axis(log_probs, token_ids.astype(jnp.int32)[:, None], axis=1)[:, 0]
    return (log_probs, chosen)
```

```python
import jax
import jax.numpy as jnp
from jax import lax
from jax.sharding import PartitionSpec as P

D = 8192
RD = 4096
Z = 8
CHUNK = 48
F32 = jnp.float32
BF16 = jnp.bfloat16


def send_z(value, step):
    return lax.ppermute(value, "wa", [(i, (i + step) % Z) for i in range(Z)])


def send_v(value, dy, dx, dc):
    pairs = []
    for i in range(32):
        y, x, c = i // 8, (i // 2) % 4, i % 2
        pairs.append((i, (((y + dy) % 4) * 4 + (x + dx) % 4) * 2 + (c ^ dc)))
    return lax.ppermute(value, "vert", pairs)


def scatter_sum_z(chunks):
    half = chunks[4].shape[-1] // 2
    far_right = send_z(chunks[4][:, :half], 2)
    far_left = send_z(chunks[4][:, half:], -2)
    mid_right = send_z(chunks[3], 1)
    mid_left = send_z(chunks[5], -1)
    near_right = send_z(chunks[1], 1)
    near_left = send_z(chunks[7], -1)
    right = chunks[2].astype(F32) + mid_right.astype(F32)
    right = jnp.concatenate([right[:, :half] + far_right.astype(F32), right[:, half:]], axis=1)
    left = chunks[6].astype(F32) + mid_left.astype(F32)
    left = jnp.concatenate([left[:, :half], left[:, half:] + far_left.astype(F32)], axis=1)
    from_right = send_z(right.astype(BF16), 2)
    from_left = send_z(left.astype(BF16), -2)
    total = chunks[0].astype(F32) + near_right.astype(F32) + near_left.astype(F32)
    return total + from_right.astype(F32) + from_left.astype(F32)


def gather_z(mine):
    half = mine.shape[0] // 2
    at = {0: mine}
    at[6] = send_z(mine, 2)
    at[2] = send_z(mine, -2)
    at[7] = send_z(mine, 1)
    at[1] = send_z(mine, -1)
    at[5] = send_z(at[6], 1)
    at[3] = send_z(at[2], -1)
    low = send_z(at[6][:half], 2)
    high = send_z(at[2][half:], -2)
    return jnp.concatenate([at[0], at[1], at[2], at[3], low, high, at[5], at[6], at[7]], axis=0)


def merge(parts):
    top = parts[0][0]
    for part in parts[1:]:
        top = jnp.maximum(top, part[0])
    terms = [jnp.exp(part[0] - top) for part in parts]
    picks = [part[1] for part in parts]
    if len(parts) == 4:
        total = (terms[0] + terms[2]) + (terms[1] + terms[3])
        pick = (picks[0] + picks[2]) + (picks[1] + picks[3])
    else:
        total = terms[0] + terms[1]
        pick = picks[0] + picks[1]
    return jnp.stack([top + jnp.log(total), pick])


def local(
    hidden_in,
    gate_levels,
    up_levels,
    gate_scale,
    up_scale,
    down_levels,
    down_scale,
    norm_gain,
    head_weight,
    reward_states,
    reward_gain,
    reward_heads,
    preference,
    token_ids,
):
    z = lax.axis_index("wa")
    vert = lax.axis_index("vert")
    x = (vert // 2) % 4
    core = vert % 2

    states = lax.all_gather(reward_states[0], "vert", axis=1, tiled=True)

    rows = lax.dynamic_slice_in_dim(jnp.concatenate([hidden_in, hidden_in], axis=0), z * CHUNK, Z * CHUNK, 0)
    gate_part = jnp.dot(rows, gate_levels, preferred_element_type=F32).astype(BF16)
    up_part = jnp.dot(rows, up_levels, preferred_element_type=F32).astype(BF16)
    both = jnp.concatenate([gate_part, up_part], axis=1)
    chunks = [both[s * CHUNK : (s + 1) * CHUNK] for s in range(Z)]
    gate_up = scatter_sum_z(chunks)
    width = gate_levels.shape[1]
    hidden = (jax.nn.silu(gate_up[:, :width] * gate_scale) * (gate_up[:, width:] * up_scale)).astype(BF16)
    hidden = gather_z(hidden)
    down_part = jnp.dot(hidden, down_levels, preferred_element_type=F32)

    keep = lax.dynamic_slice_in_dim(down_part, core * 192, 192, 0)
    give = lax.dynamic_slice_in_dim(down_part, (1 - core) * 192, 192, 0).astype(BF16)
    by_core = keep + send_v(give, 0, 0, 1).astype(F32)

    def quarter(value, d):
        return lax.dynamic_slice_in_dim(value, lax.rem(x + d, 4) * CHUNK, CHUNK, 0)

    got = [send_v(quarter(by_core, d).astype(BF16), 0, d, 0) for d in (1, 2, 3)]
    by_x = quarter(by_core, 0) + got[0].astype(F32) + got[1].astype(F32) + got[2].astype(F32)
    by_x_sent = by_x.astype(BF16)
    got = [send_v(by_x_sent, d, 0, 0) for d in (1, 2, 3)]
    down = by_x + got[0].astype(F32) + got[1].astype(F32) + got[2].astype(F32)

    own_rows = lax.dynamic_slice_in_dim(rows, core * 192 + x * CHUNK, CHUNK, 0).astype(F32)
    resid = own_rows + down * down_scale
    squares = jnp.sum(resid * resid, axis=1, keepdims=True)
    high = squares.astype(BF16)
    low = (squares - high.astype(F32)).astype(BF16)
    lane = lax.broadcasted_iota(jnp.int32, (CHUNK, 128), 1)
    tail = jnp.where(lane == 0, high, jnp.where(lane == 1, low, jnp.zeros((), BF16)))
    mine = jnp.concatenate([(resid * norm_gain).astype(BF16), tail], axis=1)

    got = [mine] + [send_v(mine, 0, -d, 0) for d in (1, 2, 3)]
    block = jnp.concatenate(got + got, axis=0)
    half = lax.dynamic_slice_in_dim(block, lax.rem(4 - x, 4) * CHUNK, 192, 0)
    other = send_v(half, 0, 0, 1)
    scaled = jnp.where(core == 0, jnp.concatenate([half, other], axis=0), jnp.concatenate([other, half], axis=0))

    columns = head_weight.shape[1]
    row_at = lax.broadcasted_iota(jnp.int32, (128, 512), 0)
    col_at = lax.broadcasted_iota(jnp.int32, (128, 512), 1)
    carry = jnp.where((row_at < 2) & (col_at == row_at + columns), 1.0, 0.0).astype(BF16)
    head = jnp.concatenate([jnp.pad(head_weight, ((0, 0), (0, 512 - columns))), carry], axis=0)
    base_part = jnp.dot(scaled, head, preferred_element_type=F32).astype(BF16)
    base_chunks = [base_part[s * CHUNK : (s + 1) * CHUNK] for s in range(Z)]

    values = states.astype(F32)
    state_scale = lax.rsqrt(jnp.mean(values * values, axis=1, keepdims=True) + 1e-05)
    reward_normed = (values * state_scale * reward_gain).astype(BF16)
    reward_logits = jnp.dot(reward_normed, reward_heads[0], preferred_element_type=F32)
    weighted = reward_logits * (preference.astype(F32) / 16.0)
    reward_rows = lax.psum_scatter(weighted, "wa", scatter_dimension=0, tiled=True)

    base_rows = scatter_sum_z(base_chunks)
    total_squares = base_rows[:, columns : columns + 1] + base_rows[:, columns + 1 : columns + 2]
    mix = base_rows[:, :columns] * lax.rsqrt(total_squares / D + 1e-05) + reward_rows

    top = jnp.max(mix, axis=1)
    local_log = top + jnp.log(jnp.sum(jnp.exp(mix - top[:, None]), axis=1))
    vocab_index = vert * columns + lax.iota(jnp.int32, columns)
    picked = jnp.sum(jnp.where(vocab_index[None, :] == token_ids[:, None], mix, 0.0), axis=1)
    state = jnp.stack([local_log, picked])
    state = merge([state, send_v(state, 0, 0, 1)])
    state = merge([state] + [send_v(state, 0, d, 0) for d in (1, 2, 3)])
    state = merge([state] + [send_v(state, d, 0, 0) for d in (1, 2, 3)])
    return (mix - state[0][:, None], state[1] - state[0])


def solution(mesh):
    return jax.shard_map(
        local,
        mesh=mesh,
        in_specs=(
            P(None, "wa"),
            P("wa", "vert"),
            P("wa", "vert"),
            P("vert"),
            P("vert"),
            P("vert", "wa"),
            P("wa"),
            P("wa"),
            P("wa", "vert"),
            P("wa", None, "vert"),
            P("wa", None),
            P("wa", None, "vert"),
            P(None, "wa"),
            P("wa"),
        ),
        out_specs=(P("wa", "vert"), P("wa")),
        check_vma=False,
    )
```
